32 devices in a mesh: dp: 4 (over y, core), cent: 8 (over z, x).
Axes of the slice: x: 2, y: 2, z: 4, core: 2. Of those that a mesh axis runs over, the one named last changes fastest.
Arguments:
- fragments: bfloat16 [8192, 1024], P(('dp', 'cent')), may hold values from -1500 to 1500
- order: int32 [32, 256], P(('dp', 'cent')), may hold values from 0 to 255, each once within a row
- group_ids: int32 [8192, 1], P(('dp', 'cent')), may hold values from 0 to 7; in each aligned block of 256 rows (0 to 255, 256 to 511, ...) at most 64 rows name the same one
- w_first: bfloat16 [1024, 1024], replicated, may hold values from -0.1875 to 0.1875
- w_second: bfloat16 [1024, 256], replicated, may hold values from -0.1875 to 0.1875
- centroids: float32 [8192, 256], P('cent'), may hold values from -24 to 24
Outputs:
- centroids_out: float32 [8192, 256], P('cent')
The draws below stay inside these ranges and needn't reach their ends.
Inputs may be any that keep to these rules, and one draw needn't show every extreme that they name: `order`: each row is a permutation of 0 to 255. `group_ids`: among the rows of one device (aligned blocks of 256 rows) no group is named by more than 64 rows, a bound that some block reaches.
All inputs are finite; a program needn't handle non-finite values.
Results may differ from the reference program's by a relative error of at most 0.0075.
Values may be sent and summed in bfloat16 or wider, within the bound.
A program may use at most 64 MiB of HBM per device.

```python
import math
import jax
import jax.numpy as jnp
import numpy as np
from jax import lax

EMB = 1024
HID = 1024
DZ = 256
CENT_DEV = 1024
STEPS = 2
ROWS_DEV = 256
ROWS = 8192
CENTROIDS = 8192
CAP = 64
N_DP = 4
N_CENT = 8


def draw_fragments(key, part):
    key_vals, key_rows, key_cols = jax.random.split(key, 3)
    row_scale = jnp.exp(jax.random.uniform(key_rows, (ROWS, 1), jnp.float32, 0.0, 2.302585))
    col_scale = jnp.exp(jax.random.uniform(key_cols, (1, EMB), jnp.float32, 0.0, 2.302585))
    device = (jnp.arange(ROWS, dtype=jnp.int32) // ROWS_DEV).astype(jnp.float32)
    count = float(max(ROWS // ROWS_DEV - 1, 1))
    ramp = (1.0 + 2.0 * device / count)[:, None]
    base = jnp.clip(jax.random.normal(key_vals, (ROWS, EMB), jnp.float32), -4.0, 4.0)
    return (base * row_scale * col_scale * ramp).astype(jnp.bfloat16)


def draw_centroids(key, part):
    key_vals, key_rows = jax.random.split(key, 2)
    base = jnp.clip(jax.random.normal(key_vals, (CENTROIDS, DZ), jnp.float32), -4.0, 4.0)
    scale = jnp.exp(jax.random.uniform(key_rows, (CENTROIDS, 1), jnp.float32, -0.693147, 0.693147))
    return base * scale


def assign_block(own_key, own, number, rows, count, top, bound, slope):
    order = jax.random.permutation(own_key, count)
    crowded, usual = portions_of(count, rows * top, bound, slope, True), portions_of(count, rows * top, bound, slope, False)
    places = jnp.arange(count)

    def named(lengths, turn):
        used = int((lengths > 0).sum())
        fixed = max(1, used // 4)
        moved = fixed + (places - fixed + turn * (used - fixed)) % max(1, count - fixed)
        return jnp.zeros((count,), jnp.int32).at[order[jnp.where(places < fixed, places, moved)]].set(jnp.asarray(lengths, jnp.int32))

    lengths = jnp.where(number % 4 == 0, named(crowded, number // 4), named(usual, number - number // 4 - 1))
    mixed = jax.random.permutation(jax.random.fold_in(own, 3), count)
    source_of, sink = mixed[0:count // 2 * 2:2], mixed[1:count // 2 * 2:2]
    margin = jnp.minimum(lengths[source_of] - 1, bound - lengths[sink]) // 2
    margin = jnp.where((source_of == order[0]) | (sink == order[0]) | (lengths[sink] == 0), 0, jnp.maximum(margin, 0))
    moved = jax.random.randint(jax.random.fold_in(own, 4), (count // 2,), 0, 1 << 20) % (margin + 1)
    lengths = lengths.at[source_of].add(-moved).at[sink].add(moved)
    items = jnp.searchsorted(jnp.cumsum(lengths), jnp.arange(rows * top), side="right").astype(jnp.int32)
    listing = items.reshape(top, rows).T
    listing = listing[jax.random.permutation(jax.random.fold_in(own, 1), rows)]
    turn = jax.random.randint(jax.random.fold_in(own, 2), (rows, 1), 0, top)
    return jnp.take_along_axis(listing, (jnp.arange(top)[None, :] + turn) % top, axis=1)


def portions_of(number_of, total, bound, skew, full):
    weights = [(1 << 20) // math.isqrt(rank ** skew) + 1 for rank in range(1, number_of + 1)]
    largest = bound if full else min(bound, max(-(-total // number_of), total * weights[0] // sum(weights)))
    least = 1 if total - largest >= number_of - 1 else 0
    counts, rest = [largest] + [least] * (number_of - 1), total - largest - least * (number_of - 1)
    while rest > 0:
        free = [i for i in range(1, number_of) if counts[i] < largest] or [i for i in range(1, number_of) if counts[i] < bound]
        mass, budget = sum([weights[i] for i in free]), rest
        for i in free:
            addition = min(bound - counts[i], max(1, budget * weights[i] // mass), rest)
            counts[i] = counts[i] + addition
            rest = rest - addition
    return np.array(counts)


def bell_draw(own_key, dims, width, bound, kind=jnp.bfloat16):
    result = width * jax.random.normal(own_key, dims, jnp.float32)
    return jnp.clip(result, min=-bound, max=bound).astype(kind)


def setup_inputs(seed: int = 0) -> dict:
    keys = jax.random.split(jax.random.key(seed), 7)
    fragments = draw_fragments(jax.random.fold_in(keys[6], 71), 0)
    order = jax.vmap(lambda own: jax.random.permutation(own, ROWS_DEV))(jax.random.split(keys[1], (ROWS // ROWS_DEV))).reshape((ROWS // ROWS_DEV, ROWS_DEV)).astype(jnp.int32)
    group_ids_keys = jax.random.split(jax.random.fold_in(keys[2], 1), ROWS // ROWS_DEV)
    group_ids_turns = jax.random.permutation(jax.random.fold_in(keys[2], 3), ROWS // ROWS_DEV)
    group_ids = jax.vmap(lambda own, number: assign_block(jax.random.fold_in(keys[2], 2), own, number, ROWS_DEV, N_CENT, 1, CAP, 1))(group_ids_keys, group_ids_turns).reshape((ROWS, 1))
    w_first = bell_draw(keys[3], (EMB, HID), EMB ** -0.5, 0.1875)
    w_second = bell_draw(keys[4], (HID, DZ), HID ** -0.5, 0.1875)
    centroids = draw_centroids(jax.random.fold_in(keys[6], 71), 0)
    return {"fragments": fragments, "order": order, "group_ids": group_ids, "w_first": w_first, "w_second": w_second, "centroids": centroids}


beta_scale = 0.0625
prior_weight = 1.0
eps_value = 1e-05

def pack_rows(zrows, groups):
    member = (groups[:, None] == jnp.arange(N_CENT, dtype=jnp.int32)[None, :]).astype(jnp.float32)
    index = jnp.arange(ROWS_DEV, dtype=jnp.int32)
    before = (index[:, None] > index[None, :]).astype(jnp.float32)
    rank = lax.optimization_barrier(jnp.sum(jnp.dot(before, member) * member, axis=1)).astype(jnp.int32)
    slot = (groups * CAP + rank).astype(jnp.int32)
    packed = jnp.zeros((N_CENT * CAP, DZ), zrows.dtype).at[slot].set(zrows)
    live = jnp.zeros((N_CENT * CAP,), jnp.float32).at[slot].set(1.0)
    return (packed, live)

def group_step(args):
    rows, live, block = args
    rounded = block.astype(jnp.bfloat16).astype(jnp.float32)
    cnorm = lax.optimization_barrier(jnp.sum(block * block, axis=1))
    cross = jnp.einsum('dsf,kf->dsk', rows.astype(jnp.float32), rounded)
    scores = beta_scale * (2.0 * cross - cnorm[None, None, :])
    top = lax.optimization_barrier(jnp.max(scores, axis=2, keepdims=True))
    expo = jnp.exp(scores - top)
    resp = expo / lax.optimization_barrier(jnp.sum(expo, axis=2, keepdims=True)) * live[:, :, None]
    resp_b = resp.astype(jnp.bfloat16).astype(jnp.float32)
    num = jnp.einsum('dsk,dsf->kf', resp_b, rows.astype(jnp.float32))
    den = lax.optimization_barrier(jnp.sum(resp_b, axis=(0, 1)))
    return (num + prior_weight * block) / (den + prior_weight)[:, None]

def reference(fragments, order, group_ids, w_first, w_second, centroids):
    devices = N_DP * N_CENT
    blocks = fragments.reshape(devices, ROWS_DEV, EMB)
    picked = jnp.take_along_axis(blocks, order.astype(jnp.int32)[:, :, None], axis=1).reshape(ROWS, EMB)
    hidden = jax.nn.gelu(jnp.dot(picked, w_first, preferred_element_type=jnp.float32), approximate=True).astype(jnp.bfloat16)
    proj = jnp.dot(hidden, w_second, preferred_element_type=jnp.float32)
    mean = lax.optimization_barrier(jnp.sum(proj, axis=0)) / ROWS
    var = lax.optimization_barrier(jnp.sum((proj - mean) ** 2, axis=0)) / ROWS
    zrows = ((proj - mean) * lax.rsqrt(var + eps_value)).astype(jnp.bfloat16)
    packed, live = jax.vmap(pack_rows)(zrows.reshape(devices, ROWS_DEV, DZ), group_ids.reshape(devices, ROWS_DEV))
    packed = packed.reshape(N_DP, N_CENT, N_CENT, CAP, DZ).transpose(2, 0, 1, 3, 4).reshape(N_CENT, N_DP, N_CENT * CAP, DZ)
    live = live.reshape(N_DP, N_CENT, N_CENT, CAP).transpose(2, 0, 1, 3).reshape(N_CENT, N_DP, N_CENT * CAP)
    current = centroids.reshape(N_CENT, CENT_DEV, DZ)
    for step in range(STEPS):
        current = lax.map(group_step, (packed, live, current))
    return current.reshape(CENTROIDS, DZ)
```

```python
import functools

import jax
import jax.numpy as jnp
from jax import lax
from jax.experimental import pallas as pl
from jax.experimental.pallas import tpu as pltpu
from jax.sharding import PartitionSpec as P

STEPS = 2
CORES = 2

beta_scale = 0.0625
prior_weight = 1.0
eps_value = 1e-05
LOG2E = 1.4426950408889634
DEAD = 1024.0
UNROLL = 8
TILE = 256

MESH = pl.DeviceIdType.MESH
NT = (((1,), (1,)), ((), ()))


def loop(n, body):
    if n <= UNROLL:
        for i in range(n):
            body(i)
    else:
        lax.fori_loop(0, n, lambda i, c: (body(i), c)[1], 0)


def kernel(
    n_dp, n_cent, cap, blocks,
    frag_hbm, order_ref, group_ref, w1_hbm, w2_hbm, cent_hbm,
    out_ref,
    frag, w1, w2, cur, proj, packed, rows, expo, live, sm_out, sm_in, st_out, st_dp, st_cent,
    in_sem, a_send, a_recv, y_send, y_recv, c_send, c_recv, s1_send, s1_recv, s2_send, s2_recv,
    sm_send, sm_recv, f_send, f_recv,
):
    dp, ce = lax.axis_index("dp"), lax.axis_index("cent")
    core = lax.rem(dp, CORES)
    n_y = n_dp // CORES
    here_y = dp // CORES
    mate = here_y * CORES + (1 - core)
    rows_here, emb = frag.shape
    hid = w1.shape[1]
    width = w2.shape[1]
    half = cur.shape[0]
    per_block = n_cent // blocks
    plane_rows = n_cent * cap

    def at(d, c):
        return {"dp": d, "cent": c}

    loads = [pltpu.make_async_copy(frag_hbm, frag, in_sem.at[0])]
    n_tiles = hid // TILE
    for j in range(n_tiles):
        cols = pl.ds(j * TILE, TILE)
        loads.append(pltpu.make_async_copy(w1_hbm.at[:, cols], w1.at[:, cols], in_sem.at[1 + j]))
    loads.append(pltpu.make_async_copy(w2_hbm, w2, in_sem.at[1 + n_tiles]))
    loads.append(pltpu.make_async_copy(cent_hbm.at[core], cur, in_sem.at[2 + n_tiles]))
    for c in loads:
        c.start()

    barrier = pltpu.get_barrier_semaphore()

    def greet_dp(k):
        pl.semaphore_signal(barrier, 1, device_id=at(lax.rem(dp + k + 1, n_dp), ce), device_id_type=MESH)

    def greet_cent(k):
        pl.semaphore_signal(barrier, 1, device_id=at(dp, lax.rem(ce + k + 1, n_cent)), device_id_type=MESH)

    loop(n_dp - 1, greet_dp)
    loop(n_cent - 1, greet_cent)

    groups = group_ref[...]
    member = lax.broadcasted_iota(jnp.int32, (max(n_cent, 16), rows_here), 0) == groups
    memberf = member.astype(jnp.float32)
    earlier = (
        lax.broadcasted_iota(jnp.int32, (rows_here, rows_here), 0)
        < lax.broadcasted_iota(jnp.int32, (rows_here, rows_here), 1)
    ).astype(jnp.float32).astype(jnp.bfloat16)
    counts = jnp.dot(memberf.astype(jnp.bfloat16), earlier, preferred_element_type=jnp.float32)
    rank = jnp.sum(counts * memberf, axis=0, keepdims=True).astype(jnp.int32)
    slot = groups * cap + rank
    place = (
        lax.broadcasted_iota(jnp.int32, (plane_rows, rows_here), 0) == slot
    ).astype(jnp.float32).astype(jnp.bfloat16)
    taken = (
        lax.broadcasted_iota(jnp.int32, (rows_here, rows_here), 0) == order_ref[...]
    ).astype(jnp.float32).astype(jnp.bfloat16)
    pickf = lax.dot_general(place, taken, NT, preferred_element_type=jnp.float32)
    pick = pickf.astype(jnp.bfloat16)
    dead = DEAD * (1.0 - jnp.sum(pickf, axis=1, keepdims=True))
    mark = jnp.where(
        lax.broadcasted_iota(jnp.int32, (plane_rows, width), 1) == 0, dead, 0.0
    )

    loads[0].wait()
    loads[1 + n_tiles].wait()
    for j in range(n_tiles):
        loads[1 + j].wait()
        h = jnp.dot(frag[...], w1[:, j * TILE:(j + 1) * TILE], preferred_element_type=jnp.float32)
        h = jax.nn.gelu(h, approximate=True).astype(jnp.bfloat16)
        p = jnp.dot(h, w2[j * TILE:(j + 1) * TILE, :], preferred_element_type=jnp.float32)
        if j == 0:
            proj[...] = p
        else:
            proj[...] += p

    pr = proj[...]
    mean = jnp.sum(pr, axis=0, keepdims=True) / rows_here
    square = jnp.sum((pr - mean) ** 2, axis=0, keepdims=True)
    st_out[0, 0:1, :] = mean
    st_out[0, 1:2, :] = square
    st_dp[dp, 0:1, :] = mean
    st_dp[dp, 1:2, :] = square

    pl.semaphore_wait(barrier, n_dp - 1 + n_cent - 1)

    def dp_copy(k):
        return pltpu.make_async_remote_copy(
            st_out.at[0], st_dp.at[dp], s1_send.at[k], s1_recv.at[k],
            device_id=at(lax.rem(dp + k + 1, n_dp), ce), device_id_type=MESH)

    def cent_copy(k):
        return pltpu.make_async_remote_copy(
            st_out.at[1], st_cent.at[ce], s2_send.at[k], s2_recv.at[k],
            device_id=at(dp, lax.rem(ce + k + 1, n_cent)), device_id_type=MESH)

    def combine(buffer, count, each):
        got = buffer[...]
        means, squares = got[:, 0, :], got[:, 1, :]
        mean = jnp.sum(means, axis=0, keepdims=True) / count
        square = jnp.sum(squares, axis=0, keepdims=True) + each * jnp.sum(
            (means - mean) ** 2, axis=0, keepdims=True)
        return mean, square

    loop(n_dp - 1, lambda k: dp_copy(k).start())
    loop(n_dp - 1, lambda k: dp_copy(k).wait_recv())
    mean, square = combine(st_dp, n_dp, float(rows_here))
    st_out[1, 0:1, :] = mean
    st_out[1, 1:2, :] = square
    st_cent[ce, 0:1, :] = mean
    st_cent[ce, 1:2, :] = square
    loop(n_cent - 1, lambda k: cent_copy(k).start())
    loop(n_cent - 1, lambda k: cent_copy(k).wait_recv())
    mean, square = combine(st_cent, n_cent, float(rows_here * n_dp))
    var = square / float(rows_here * n_dp * n_cent)
    z = ((proj[...] - mean) * lax.rsqrt(var + eps_value)).astype(jnp.bfloat16)
    full = jnp.dot(pick, z, preferred_element_type=jnp.float32) + mark
    packed[...] = full.astype(jnp.bfloat16).reshape(n_cent, cap, width)

    def a_copy(k):
        peer = lax.rem(ce + k + 1, n_cent)
        return pltpu.make_async_remote_copy(
            packed.at[peer], rows.at[dp, ce], a_send.at[peer], a_recv.at[ce],
            device_id=at(dp, peer), device_id_type=MESH)

    def a_arrival(src):
        return pltpu.make_async_copy(packed.at[src], rows.at[dp, src], a_recv.at[src])

    a_arrival(ce).start()
    loop(n_cent - 1, lambda k: a_copy(k).start())

    def part(plane, b):
        return rows.at[plane, pl.ds(b * per_block, per_block)]

    def y_copy(k, b):
        return pltpu.make_async_remote_copy(
            part(dp, b), part(dp, b), y_send.at[k, b], y_recv.at[k, b],
            device_id=at(lax.rem(here_y + k, n_y) * CORES + core, ce), device_id_type=MESH)

    def plane_of(k, which):
        return lax.rem(here_y + n_y - k, n_y) * CORES + which

    def y_arrival(k, b):
        plane = plane_of(k, core)
        return pltpu.make_async_copy(part(plane, b), part(plane, b), y_recv.at[k, b])

    def c_copy(k, b):
        plane = plane_of(k, core)
        return pltpu.make_async_remote_copy(
            part(plane, b), part(plane, b), c_send.at[k, b], c_recv.at[k, b],
            device_id=at(mate, ce), device_id_type=MESH)

    mine = ce // per_block
    for i in range(blocks):
        b = lax.rem(mine + blocks - i, blocks)
        loop(per_block, lambda q: a_arrival(b * per_block + q).wait())
        for k in range(1, n_y):
            y_copy(k, b).start()
        c_copy(0, b).start()

    loads[2 + n_tiles].wait()
    selector = (
        (lax.broadcasted_iota(jnp.int32, (16, width), 0) == 0)
        & (lax.broadcasted_iota(jnp.int32, (16, width), 1) == 0)
    ).astype(jnp.float32).astype(jnp.bfloat16)

    def sm_copy(step, plane):
        return pltpu.make_async_remote_copy(
            sm_out.at[step, plane], sm_in.at[step, plane],
            sm_send.at[step, plane], sm_recv.at[step, plane],
            device_id=at(mate, ce), device_id_type=MESH)

    n_sub = plane_rows // TILE
    sub_cents = TILE // cap

    def sub_rows(plane, t):
        return rows[plane, t * sub_cents:(t + 1) * sub_cents].reshape(TILE, width)

    def first_pass(step, plane, rounded, cnorm):
        for t in range(n_sub):
            lanes = slice(t * TILE, (t + 1) * TILE)
            x = sub_rows(plane, t)
            if step == 0:
                flag = lax.dot_general(selector, x, NT, preferred_element_type=jnp.float32)
                live[plane, :, lanes] = (flag[0:1] < 0.5 * DEAD).astype(jnp.float32)
            s = lax.dot_general(rounded, x, NT, preferred_element_type=jnp.float32)
            s = s * (2.0 * beta_scale * LOG2E) - cnorm
            top = jnp.max(s, axis=0, keepdims=True)
            e = jnp.exp2(s - top)
            expo[plane, :, lanes] = e
            sm_out[step, plane, 0:1, lanes] = top
            sm_out[step, plane, 1:2, lanes] = jnp.sum(e, axis=0, keepdims=True)
        sm_copy(step, plane).start()

    def second_pass(step, plane, first, num, den):
        sm_copy(step, plane).wait_recv()
        for t in range(n_sub):
            lanes = slice(t * TILE, (t + 1) * TILE)
            m0, s0 = sm_out[step, plane, 0:1, lanes], sm_out[step, plane, 1:2, lanes]
            m1, s1 = sm_in[step, plane, 0:1, lanes], sm_in[step, plane, 1:2, lanes]
            top = jnp.maximum(m0, m1)
            own = jnp.exp2(m0 - top)
            total = s0 * own + s1 * jnp.exp2(m1 - top)
            r = (expo[plane, :, lanes] * (own / total * live[plane, :, lanes])).astype(jnp.bfloat16)
            num = num + jnp.dot(r, sub_rows(plane, t), preferred_element_type=jnp.float32)
            den = den + jnp.sum(r.astype(jnp.float32), axis=1, keepdims=True)
        return num, den

    def all_planes(body, carry):
        if n_dp <= UNROLL:
            for k in range(n_y):
                for other in range(CORES):
                    carry = body(plane_of(k, core if other == 0 else 1 - core), carry)
            return carry
        return lax.fori_loop(
            0, n_dp, lambda i, c: body(plane_of(i // CORES, lax.rem(core + i, CORES)), c), carry)

    for step in range(STEPS):
        current = cur[...]
        rounded = current.astype(jnp.bfloat16)
        cnorm = (beta_scale * LOG2E) * jnp.sum(current * current, axis=1, keepdims=True)
        if step == 0:
            first_pass(step, plane_of(0, core), rounded, cnorm)
            for i in range(blocks):
                c_copy(0, lax.rem(mine + blocks - i, blocks)).wait_recv()
            first_pass(step, plane_of(0, 1 - core), rounded, cnorm)
            for k in range(1, n_y):
                for i in range(blocks):
                    b = lax.rem(mine + blocks - i, blocks)
                    y_arrival(k, b).wait()
                    c_copy(k, b).start()
                first_pass(step, plane_of(k, core), rounded, cnorm)
                for i in range(blocks):
                    c_copy(k, lax.rem(mine + blocks - i, blocks)).wait_recv()
                first_pass(step, plane_of(k, 1 - core), rounded, cnorm)
        else:
            all_planes(lambda plane, c: (first_pass(step, plane, rounded, cnorm), c)[1], 0)
        num = jnp.zeros((half, width), jnp.float32)
        den = jnp.zeros((half, 1), jnp.float32)
        num, den = all_planes(
            lambda plane, c: second_pass(step, plane, False, c[0], c[1]), (num, den))
        fresh = (num + prior_weight * cur[...]) / (den + prior_weight)
        if step < STEPS - 1:
            cur[...] = fresh
        else:
            out_ref[core] = fresh

    final = pltpu.make_async_remote_copy(
        out_ref.at[core], out_ref.at[core], f_send, f_recv,
        device_id=at(mate, ce), device_id_type=MESH)
    final.start()
    loop(n_dp - 1, lambda k: dp_copy(k).wait_send())
    loop(n_cent - 1, lambda k: cent_copy(k).wait_send())
    loop(n_cent - 1, lambda k: a_copy(k).wait_send())
    for k in range(n_y):
        for b in range(blocks):
            if k:
                y_copy(k, b).wait_send()
            c_copy(k, b).wait_send()
    for step in range(STEPS):
        loop(n_dp, lambda plane: sm_copy(step, plane).wait_send())
    final.wait()


def per_device(fragments, order, group_ids, w_first, w_second, centroids):
    rows_here, emb = fragments.shape
    hid, width = w_second.shape
    n_dp, n_cent = lax.axis_size("dp"), lax.axis_size("cent")
    n_y = n_dp // CORES
    cap = max(16, 2 * rows_here // n_cent)
    plane_rows = n_cent * cap
    blocks = min(n_cent, 8)
    half = centroids.shape[0] // CORES
    n_tiles = hid // TILE
    f32, bf16 = jnp.float32, jnp.bfloat16
    dma = pltpu.SemaphoreType.DMA
    vmem = pl.BlockSpec(memory_space=pltpu.VMEM)
    anyspace = pl.BlockSpec(memory_space=pl.ANY)
    need = 2 * (emb * hid + rows_here * emb + n_dp * plane_rows * width) + 4 * n_dp * plane_rows * half
    out = pl.pallas_call(
        functools.partial(kernel, n_dp, n_cent, cap, blocks),
        out_shape=jax.ShapeDtypeStruct((CORES, half, width), f32),
        in_specs=[anyspace, vmem, vmem, anyspace, anyspace, anyspace],
        out_specs=vmem,
        scratch_shapes=[
            pltpu.VMEM((rows_here, emb), bf16),
            pltpu.VMEM((emb, hid), bf16),
            pltpu.VMEM((hid, width), bf16),
            pltpu.VMEM((half, width), f32),
            pltpu.VMEM((rows_here, width), f32),
            pltpu.VMEM((n_cent, cap, width), bf16),
            pltpu.VMEM((n_dp, n_cent, cap, width), bf16),
            pltpu.VMEM((n_dp, half, plane_rows), f32),
            pltpu.VMEM((n_dp, 1, plane_rows), f32),
            pltpu.VMEM((STEPS, n_dp, 2, plane_rows), f32),
            pltpu.VMEM((STEPS, n_dp, 2, plane_rows), f32),
            pltpu.VMEM((2, 2, width), f32),
            pltpu.VMEM((n_dp, 2, width), f32),
            pltpu.VMEM((n_cent, 2, width), f32),
            dma((3 + n_tiles,)),
            dma((n_cent,)), dma((n_cent,)),
            dma((n_y, blocks)), dma((n_y, blocks)),
            dma((n_y, blocks)), dma((n_y, blocks)),
            dma((n_dp,)), dma((n_dp,)),
            dma((n_cent,)), dma((n_cent,)),
            dma((STEPS, n_dp)), dma((STEPS, n_dp)),
            dma, dma,
        ],
        compiler_params=pltpu.CompilerParams(
            collective_id=0, has_side_effects=True, vmem_limit_bytes=min(58 << 20, need + (14 << 20))
        ),
    )(
        fragments, order, group_ids.reshape(1, rows_here), w_first, w_second,
        centroids.reshape(CORES, half, width),
    )
    return out.reshape(CORES * half, width)


def solution(mesh):
    return jax.shard_map(
        per_device,
        mesh=mesh,
        in_specs=(
            P(("dp", "cent"), None),
            P(("dp", "cent"), None),
            P(("dp", "cent"), None),
            P(),
            P(),
            P("cent", None),
        ),
        out_specs=P("cent", None),
        check_vma=False,
    )
```

```python
import functools

import jax
import jax.numpy as jnp
from jax import lax
from jax.experimental import pallas as pl
from jax.experimental.pallas import tpu as pltpu
from jax.sharding import PartitionSpec as P

STEPS = 2
CORES = 2

beta_scale = 0.0625
prior_weight = 1.0
eps_value = 1e-05
LOG2E = 1.4426950408889634
DEAD = 1024.0
UNROLL = 8
TILE = 256
VMEM_BYTES = 60 << 20

MESH = pl.DeviceIdType.MESH
NT = (((1,), (1,)), ((), ()))


def loop(n, body):
    if n <= UNROLL:
        for i in range(n):
            body(i)
    else:
        lax.fori_loop(0, n, lambda i, c: (body(i), c)[1], 0)


def kernel(
    n_dp, n_cent, cap, blocks,
    frag_hbm, order_hbm, group_hbm, w1_hbm, w2_hbm, cent_hbm,
    out_ref,
    frag, order_ref, group_ref, w1, w2, cur, proj, packed, rows, zrows, expo, live, sm_out, sm_in, stats,
    in_sem, a_send, a_recv, y_send, y_recv, c_send, c_recv, s1_send, s1_recv, s2_send, s2_recv,
    sm_send, sm_recv, f_send, f_recv,
):
    dp, ce = lax.axis_index("dp"), lax.axis_index("cent")
    core = lax.rem(dp, CORES)
    n_y = n_dp // CORES
    here_y = dp // CORES
    mate = here_y * CORES + (1 - core)
    rows_here, emb = frag.shape
    hid = w1.shape[1]
    width = w2.shape[1]
    half = cur.shape[0]
    per_block = n_cent // blocks
    plane_rows = n_cent * cap

    def at(d, c):
        return {"dp": d, "cent": c}

    n_tiles = hid // TILE
    small = [
        pltpu.make_async_copy(group_hbm, group_ref, in_sem.at[3 + n_tiles]),
        pltpu.make_async_copy(order_hbm, order_ref, in_sem.at[4 + n_tiles]),
    ]
    loads = [pltpu.make_async_copy(frag_hbm, frag, in_sem.at[0])]
    for j in range(n_tiles):
        cols = pl.ds(j * TILE, TILE)
        loads.append(pltpu.make_async_copy(w1_hbm.at[:, cols], w1.at[:, cols], in_sem.at[1 + j]))
    loads.append(pltpu.make_async_copy(w2_hbm, w2, in_sem.at[1 + n_tiles]))
    loads.append(pltpu.make_async_copy(cent_hbm.at[core], cur, in_sem.at[2 + n_tiles]))
    for c in small + loads:
        c.start()

    barrier = pltpu.get_barrier_semaphore()

    def greet_dp(k):
        pl.semaphore_signal(barrier, 1, device_id=at(lax.rem(dp + k + 1, n_dp), ce), device_id_type=MESH)

    def greet_cent(k):
        pl.semaphore_signal(barrier, 1, device_id=at(dp, lax.rem(ce + k + 1, n_cent)), device_id_type=MESH)

    loop(n_dp - 1, greet_dp)
    loop(n_cent - 1, greet_cent)

    for c in small:
        c.wait()
    groups = group_ref[...]
    member = lax.broadcasted_iota(jnp.int32, (max(n_cent, 16), rows_here), 0) == groups
    memberf = member.astype(jnp.float32)
    earlier = (
        lax.broadcasted_iota(jnp.int32, (rows_here, rows_here), 0)
        < lax.broadcasted_iota(jnp.int32, (rows_here, rows_here), 1)
    ).astype(jnp.float32).astype(jnp.bfloat16)
    counts = jnp.dot(memberf.astype(jnp.bfloat16), earlier, preferred_element_type=jnp.float32)
    rank = jnp.sum(counts * memberf, axis=0, keepdims=True).astype(jnp.int32)
    slot = groups * cap + rank
    place = (
        lax.broadcasted_iota(jnp.int32, (plane_rows, rows_here), 0) == slot
    ).astype(jnp.float32).astype(jnp.bfloat16)
    taken = (
        lax.broadcasted_iota(jnp.int32, (rows_here, rows_here), 0) == order_ref[...]
    ).astype(jnp.float32).astype(jnp.bfloat16)
    pickf = lax.dot_general(place, taken, NT, preferred_element_type=jnp.float32)
    pick = pickf.astype(jnp.bfloat16)
    dead = DEAD * (1.0 - jnp.sum(pickf, axis=1, keepdims=True))
    mark = jnp.where(
        lax.broadcasted_iota(jnp.int32, (plane_rows, width), 1) == 0, dead, 0.0
    )

    loads[0].wait()
    loads[1 + n_tiles].wait()
    for j in range(n_tiles):
        loads[1 + j].wait()
        h = jnp.dot(frag[...], w1[:, j * TILE:(j + 1) * TILE], preferred_element_type=jnp.float32)
        h = jax.nn.gelu(h, approximate=True).astype(jnp.bfloat16)
        p = jnp.dot(h, w2[j * TILE:(j + 1) * TILE, :], preferred_element_type=jnp.float32)
        if j == 0:
            proj[...] = p
        else:
            proj[...] += p

    pr = proj[...]
    mean = jnp.sum(pr, axis=0, keepdims=True) / rows_here
    centered = pr - mean
    square = jnp.sum(centered * centered, axis=0, keepdims=True)
    stats[ce, dp, 0:1, :] = mean
    stats[ce, dp, 1:2, :] = square
    z = (centered * lax.rsqrt(square / rows_here + eps_value)).astype(jnp.bfloat16)
    full = jnp.dot(pick, z, preferred_element_type=jnp.float32) + mark
    packed[...] = full.astype(jnp.bfloat16).reshape(n_cent, cap, width)

    pl.semaphore_wait(barrier, n_dp - 1 + n_cent - 1)

    def dp_copy(k):
        return pltpu.make_async_remote_copy(
            stats.at[ce, dp], stats.at[ce, dp], s1_send.at[k], s1_recv.at[k],
            device_id=at(lax.rem(dp + k + 1, n_dp), ce), device_id_type=MESH)

    def cent_copy(k):
        return pltpu.make_async_remote_copy(
            stats.at[ce], stats.at[ce], s2_send.at[k], s2_recv.at[k],
            device_id=at(dp, lax.rem(ce + k + 1, n_cent)), device_id_type=MESH)

    loop(n_dp - 1, lambda k: dp_copy(k).start())

    def a_copy(k):
        peer = lax.rem(ce + k + 1, n_cent)
        return pltpu.make_async_remote_copy(
            packed.at[peer], rows.at[dp, ce], a_send.at[peer], a_recv.at[ce],
            device_id=at(dp, peer), device_id_type=MESH)

    def a_arrival(src):
        return pltpu.make_async_copy(packed.at[src], rows.at[dp, src], a_recv.at[src])

    a_arrival(ce).start()
    loop(n_cent - 1, lambda k: a_copy(k).start())
    loop(n_dp - 1, lambda k: dp_copy(k).wait_recv())
    loop(n_cent - 1, lambda k: cent_copy(k).start())

    def part(plane, b):
        return rows.at[plane, pl.ds(b * per_block, per_block)]

    def y_copy(k, b):
        return pltpu.make_async_remote_copy(
            part(dp, b), part(dp, b), y_send.at[k, b], y_recv.at[k, b],
            device_id=at(lax.rem(here_y + k, n_y) * CORES + core, ce), device_id_type=MESH)

    def plane_of(k, which):
        return lax.rem(here_y + n_y - k, n_y) * CORES + which

    def y_arrival(k, b):
        plane = plane_of(k, core)
        return pltpu.make_async_copy(part(plane, b), part(plane, b), y_recv.at[k, b])

    def c_copy(k, b):
        plane = plane_of(k, core)
        return pltpu.make_async_remote_copy(
            part(plane, b), part(plane, b), c_send.at[k, b], c_recv.at[k, b],
            device_id=at(mate, ce), device_id_type=MESH)

    mine = ce // per_block
    for i in range(blocks):
        b = lax.rem(mine + blocks - i, blocks)
        loop(per_block, lambda q: a_arrival(b * per_block + q).wait())
        for k in range(1, n_y):
            y_copy(k, b).start()
        c_copy(0, b).start()

    loop(n_cent - 1, lambda k: cent_copy(k).wait_recv())
    got = stats[...]
    total = jnp.sum(got, axis=(0, 1))
    mean = total[0:1] / (n_dp * n_cent)
    apart = jnp.sum((got - mean) ** 2, axis=(0, 1))
    var = (total[1:2] + rows_here * apart[0:1]) / float(rows_here * n_dp * n_cent)
    inverse = lax.rsqrt(var + eps_value)

    loads[2 + n_tiles].wait()
    selector = (
        (lax.broadcasted_iota(jnp.int32, (16, width), 0) == 0)
        & (lax.broadcasted_iota(jnp.int32, (16, width), 1) == 0)
    ).astype(jnp.float32).astype(jnp.bfloat16)

    def sm_copy(step, plane):
        return pltpu.make_async_remote_copy(
            sm_out.at[step, plane], sm_in.at[step, plane],
            sm_send.at[step, plane], sm_recv.at[step, plane],
            device_id=at(mate, ce), device_id_type=MESH)

    n_sub = plane_rows // TILE
    sub_cents = TILE // cap

    def sub_rows(plane, t):
        return zrows[plane, t * TILE:(t + 1) * TILE]

    def normalise(plane, t):
        part = slice(t * sub_cents, (t + 1) * sub_cents)
        raw = rows[plane, part]
        own = stats[part, plane]
        scale = jnp.sqrt(own[:, 1:2] / rows_here + eps_value) * inverse
        shift = (own[:, 0:1] - mean) * inverse
        x = (raw.astype(jnp.float32) * scale + shift).astype(jnp.bfloat16)
        zrows[plane, t * TILE:(t + 1) * TILE] = x.reshape(TILE, width)
        flag = lax.dot_general(
            selector, raw.reshape(TILE, width), NT, preferred_element_type=jnp.float32)
        live[plane, :, t * TILE:(t + 1) * TILE] = (flag[0:1] < 0.5 * DEAD).astype(jnp.float32)

    def first_pass(step, plane, rounded, cnorm):
        for t in range(n_sub):
            lanes = slice(t * TILE, (t + 1) * TILE)
            if step == 0:
                normalise(plane, t)
            x = sub_rows(plane, t)
            s = lax.dot_general(rounded, x, NT, preferred_element_type=jnp.float32)
            s = s * (2.0 * beta_scale * LOG2E) - cnorm
            top = jnp.max(s, axis=0, keepdims=True)
            e = jnp.exp2(s - top)
            expo[plane, :, lanes] = e
            sm_out[step, plane, 0:1, lanes] = top
            sm_out[step, plane, 1:2, lanes] = jnp.sum(e, axis=0, keepdims=True)
        sm_copy(step, plane).start()

    def second_pass(step, plane, first, num, den):
        sm_copy(step, plane).wait_recv()
        for t in range(n_sub):
            lanes = slice(t * TILE, (t + 1) * TILE)
            m0, s0 = sm_out[step, plane, 0:1, lanes], sm_out[step, plane, 1:2, lanes]
            m1, s1 = sm_in[step, plane, 0:1, lanes], sm_in[step, plane, 1:2, lanes]
            top = jnp.maximum(m0, m1)
            own = jnp.exp2(m0 - top)
            total = s0 * own + s1 * jnp.exp2(m1 - top)
            r = (expo[plane, :, lanes] * (own / total * live[plane, :, lanes])).astype(jnp.bfloat16)
            num = num + jnp.dot(r, sub_rows(plane, t), preferred_element_type=jnp.float32)
            den = den + jnp.sum(r.astype(jnp.float32), axis=1, keepdims=True)
        return num, den

    def all_planes(body, carry):
        if n_dp <= UNROLL:
            for k in range(n_y):
                for other in range(CORES):
                    carry = body(plane_of(k, core if other == 0 else 1 - core), carry)
            return carry
        return lax.fori_loop(
            0, n_dp, lambda i, c: body(plane_of(i // CORES, lax.rem(core + i, CORES)), c), carry)

    for step in range(STEPS):
        current = cur[...]
        rounded = current.astype(jnp.bfloat16)
        cnorm = (beta_scale * LOG2E) * jnp.sum(current * current, axis=1, keepdims=True)
        if step == 0:
            first_pass(step, plane_of(0, core), rounded, cnorm)
            for i in range(blocks):
                c_copy(0, lax.rem(mine + blocks - i, blocks)).wait_recv()
            first_pass(step, plane_of(0, 1 - core), rounded, cnorm)
            for k in range(1, n_y):
                for i in range(blocks):
                    b = lax.rem(mine + blocks - i, blocks)
                    y_arrival(k, b).wait()
                    c_copy(k, b).start()
                first_pass(step, plane_of(k, core), rounded, cnorm)
                for i in range(blocks):
                    c_copy(k, lax.rem(mine + blocks - i, blocks)).wait_recv()
                first_pass(step, plane_of(k, 1 - core), rounded, cnorm)
        else:
            all_planes(lambda plane, c: (first_pass(step, plane, rounded, cnorm), c)[1], 0)
        num = jnp.zeros((half, width), jnp.float32)
        den = jnp.zeros((half, 1), jnp.float32)
        num, den = all_planes(
            lambda plane, c: second_pass(step, plane, False, c[0], c[1]), (num, den))
        fresh = (num + prior_weight * cur[...]) / (den + prior_weight)
        if step < STEPS - 1:
            cur[...] = fresh
        else:
            out_ref[core] = fresh

    final = pltpu.make_async_remote_copy(
        out_ref.at[core], out_ref.at[core], f_send, f_recv,
        device_id=at(mate, ce), device_id_type=MESH)
    final.start()
    loop(n_dp - 1, lambda k: dp_copy(k).wait_send())
    loop(n_cent - 1, lambda k: cent_copy(k).wait_send())
    loop(n_cent - 1, lambda k: a_copy(k).wait_send())
    for k in range(n_y):
        for b in range(blocks):
            if k:
                y_copy(k, b).wait_send()
            c_copy(k, b).wait_send()
    for step in range(STEPS):
        loop(n_dp, lambda plane: sm_copy(step, plane).wait_send())
    final.wait()


def per_device(fragments, order, group_ids, w_first, w_second, centroids):
    rows_here, emb = fragments.shape
    hid, width = w_second.shape
    n_dp, n_cent = lax.axis_size("dp"), lax.axis_size("cent")
    n_y = n_dp // CORES
    cap = max(16, 2 * rows_here // n_cent)
    plane_rows = n_cent * cap
    blocks = min(n_cent, 8)
    half = centroids.shape[0] // CORES
    n_tiles = hid // TILE
    f32, bf16 = jnp.float32, jnp.bfloat16
    dma = pltpu.SemaphoreType.DMA
    vmem = pl.BlockSpec(memory_space=pltpu.VMEM)
    hbm = pl.BlockSpec(memory_space=pltpu.HBM)
    out = pl.pallas_call(
        functools.partial(kernel, n_dp, n_cent, cap, blocks),
        out_shape=jax.ShapeDtypeStruct((CORES, half, width), f32),
        in_specs=[hbm] * 6,
        out_specs=vmem,
        scratch_shapes=[
            pltpu.VMEM((rows_here, emb), bf16),
            pltpu.VMEM((1, rows_here), jnp.int32),
            pltpu.VMEM((1, rows_here), jnp.int32),
            pltpu.VMEM((emb, hid), bf16),
            pltpu.VMEM((hid, width), bf16),
            pltpu.VMEM((half, width), f32),
            pltpu.VMEM((rows_here, width), f32),
            pltpu.VMEM((n_cent, cap, width), bf16),
            pltpu.VMEM((n_dp, n_cent, cap, width), bf16),
            pltpu.VMEM((n_dp, plane_rows, width), bf16),
            pltpu.VMEM((n_dp, half, plane_rows), f32),
            pltpu.VMEM((n_dp, 1, plane_rows), f32),
            pltpu.VMEM((STEPS, n_dp, 2, plane_rows), f32),
            pltpu.VMEM((STEPS, n_dp, 2, plane_rows), f32),
            pltpu.VMEM((n_cent, n_dp, 2, width), f32),
            dma((5 + n_tiles,)),
            dma((n_cent,)), dma((n_cent,)),
            dma((n_y, blocks)), dma((n_y, blocks)),
            dma((n_y, blocks)), dma((n_y, blocks)),
            dma((n_dp,)), dma((n_dp,)),
            dma((n_cent,)), dma((n_cent,)),
            dma((STEPS, n_dp)), dma((STEPS, n_dp)),
            dma, dma,
        ],
        compiler_params=pltpu.CompilerParams(
            collective_id=0, has_side_effects=True, vmem_limit_bytes=VMEM_BYTES
        ),
    )(
        fragments, order, group_ids.reshape(1, rows_here), w_first, w_second,
        centroids.reshape(CORES, half, width),
    )
    return out.reshape(CORES * half, width)


def solution(mesh):
    return jax.shard_map(
        per_device,
        mesh=mesh,
        in_specs=(
            P(("dp", "cent"), None),
            P(("dp", "cent"), None),
            P(("dp", "cent"), None),
            P(),
            P(),
            P("cent", None),
        ),
        out_specs=P("cent", None),
        check_vma=False,
    )
```

```python
import functools

import jax
import jax.numpy as jnp
from jax import lax
from jax.experimental import pallas as pl
from jax.experimental.pallas import tpu as pltpu
from jax.sharding import PartitionSpec as P

STEPS = 2
CORES = 2

beta_scale = 0.0625
prior_weight = 1.0
eps_value = 1e-05
LOG2E = 1.4426950408889634
DEAD = 1024.0
UNROLL = 8
TILE = 256
FINAL = 2
VMEM_BYTES = 60 << 20

MESH = pl.DeviceIdType.MESH
NT = (((1,), (1,)), ((), ()))


def loop(n, body):
    if n <= UNROLL:
        for i in range(n):
            body(i)
    else:
        lax.fori_loop(0, n, lambda i, c: (body(i), c)[1], 0)


def offsets(n_dp, n_cent):
    return [(a, b) for b in range(n_cent) for a in range(n_dp) if a or b]


def kernel(
    n_dp, n_cent, cap, blocks,
    frag_hbm, order_hbm, group_hbm, w1_hbm, w2_hbm, cent_hbm,
    out_ref,
    frag, order_ref, group_ref, w1, w2, cur, proj, packed, rows, zrows, expo, live, sm_out, sm_in, stats,
    in_sem, a_send, a_recv, y_send, y_recv, c_send, c_recv, s1_send, s1_recv, s2_send, s2_recv,
    sm_send, sm_recv, f_send, f_recv, k_sem,
):
    dp, ce = lax.axis_index("dp"), lax.axis_index("cent")
    core = lax.rem(dp, CORES)
    n_y = n_dp // CORES
    here_y = dp // CORES
    mate = here_y * CORES + (1 - core)
    rows_here, emb = frag.shape
    hid = w1.shape[1]
    width = w2.shape[1]
    half = cur.shape[0]
    per_block = n_cent // blocks
    plane_rows = n_cent * cap

    def at(d, c):
        return {"dp": d, "cent": c}

    n_tiles = hid // TILE
    small = [
        pltpu.make_async_copy(group_hbm, group_ref, in_sem.at[3 + n_tiles]),
        pltpu.make_async_copy(order_hbm, order_ref, in_sem.at[4 + n_tiles]),
    ]
    loads = [pltpu.make_async_copy(frag_hbm, frag, in_sem.at[0])]
    for j in range(n_tiles):
        cols = pl.ds(j * TILE, TILE)
        loads.append(pltpu.make_async_copy(w1_hbm.at[:, cols], w1.at[:, cols], in_sem.at[1 + j]))
    loads.append(pltpu.make_async_copy(w2_hbm, w2, in_sem.at[1 + n_tiles]))
    loads.append(pltpu.make_async_copy(cent_hbm.at[core], cur, in_sem.at[2 + n_tiles]))
    for c in small + loads:
        c.start()

    barrier = pltpu.get_barrier_semaphore()

    def greet_dp(k):
        pl.semaphore_signal(barrier, 1, device_id=at(lax.rem(dp + k + 1, n_dp), ce), device_id_type=MESH)

    def greet_cent(k):
        pl.semaphore_signal(barrier, 1, device_id=at(dp, lax.rem(ce + k + 1, n_cent)), device_id_type=MESH)

    direct = s1_send.shape[0] == n_dp * n_cent
    if direct:
        greeted = n_dp * n_cent - 1
        for a, b in offsets(n_dp, n_cent):
            pl.semaphore_signal(
                barrier, 1, device_id=at(lax.rem(dp + a, n_dp), lax.rem(ce + b, n_cent)),
                device_id_type=MESH)
    else:
        greeted = n_dp - 1 + n_cent - 1
        loop(n_dp - 1, greet_dp)
        loop(n_cent - 1, greet_cent)

    for c in small:
        c.wait()
    groups = group_ref[...]
    member = lax.broadcasted_iota(jnp.int32, (max(n_cent, 16), rows_here), 0) == groups
    memberf = member.astype(jnp.float32)
    earlier = (
        lax.broadcasted_iota(jnp.int32, (rows_here, rows_here), 0)
        < lax.broadcasted_iota(jnp.int32, (rows_here, rows_here), 1)
    ).astype(jnp.float32).astype(jnp.bfloat16)
    counts = jnp.dot(memberf.astype(jnp.bfloat16), earlier, preferred_element_type=jnp.float32)
    rank = jnp.sum(counts * memberf, axis=0, keepdims=True).astype(jnp.int32)
    slot = groups * cap + rank
    place = (
        lax.broadcasted_iota(jnp.int32, (plane_rows, rows_here), 0) == slot
    ).astype(jnp.float32).astype(jnp.bfloat16)
    taken = (
        lax.broadcasted_iota(jnp.int32, (rows_here, rows_here), 0) == order_ref[...]
    ).astype(jnp.float32).astype(jnp.bfloat16)
    pickf = lax.dot_general(place, taken, NT, preferred_element_type=jnp.float32)
    pick = pickf.astype(jnp.bfloat16)
    dead = DEAD * (1.0 - jnp.sum(pickf, axis=1, keepdims=True))
    mark = jnp.where(
        lax.broadcasted_iota(jnp.int32, (plane_rows, width), 1) == 0, dead, 0.0
    )

    loads[0].wait()
    loads[1 + n_tiles].wait()
    for j in range(n_tiles):
        loads[1 + j].wait()
        h = jnp.dot(frag[...], w1[:, j * TILE:(j + 1) * TILE], preferred_element_type=jnp.float32)
        h = jax.nn.gelu(h, approximate=True).astype(jnp.bfloat16)
        p = jnp.dot(h, w2[j * TILE:(j + 1) * TILE, :], preferred_element_type=jnp.float32)
        if j == 0:
            proj[...] = p
        else:
            proj[...] += p

    pr = proj[...]
    mean = jnp.sum(pr, axis=0, keepdims=True) / rows_here
    centered = pr - mean
    square = jnp.sum(centered * centered, axis=0, keepdims=True)
    stats[ce, dp, 0:1, :] = mean
    stats[ce, dp, 1:2, :] = square
    z = (centered * lax.rsqrt(square / rows_here + eps_value)).astype(jnp.bfloat16)
    full = jnp.dot(pick, z, preferred_element_type=jnp.float32) + mark
    packed[...] = full.astype(jnp.bfloat16).reshape(n_cent, cap, width)

    pl.semaphore_wait(barrier, greeted)

    def dp_copy(k):
        return pltpu.make_async_remote_copy(
            stats.at[ce, dp], stats.at[ce, dp], s1_send.at[k], s1_recv.at[k],
            device_id=at(lax.rem(dp + k + 1, n_dp), ce), device_id_type=MESH)

    def cent_copy(k):
        return pltpu.make_async_remote_copy(
            stats.at[ce], stats.at[ce], s2_send.at[k], s2_recv.at[k],
            device_id=at(dp, lax.rem(ce + k + 1, n_cent)), device_id_type=MESH)

    def all_copy(a, b):
        return pltpu.make_async_remote_copy(
            stats.at[ce, dp], stats.at[ce, dp], s1_send.at[a * n_cent + b], s1_recv.at[a * n_cent + b],
            device_id=at(lax.rem(dp + a, n_dp), lax.rem(ce + b, n_cent)), device_id_type=MESH)


    def a_copy(k):
        peer = lax.rem(ce + k + 1, n_cent)
        return pltpu.make_async_remote_copy(
            packed.at[peer], rows.at[dp, ce], a_send.at[peer], a_recv.at[ce],
            device_id=at(dp, peer), device_id_type=MESH)

    def a_arrival(src):
        return pltpu.make_async_copy(packed.at[src], rows.at[dp, src], a_recv.at[src])

    a_arrival(ce).start()
    loop(n_cent - 1, lambda k: a_copy(k).start())
    if not direct:
        loop(n_dp - 1, lambda k: dp_copy(k).start())
        loop(n_dp - 1, lambda k: dp_copy(k).wait_recv())
        loop(n_cent - 1, lambda k: cent_copy(k).start())

    def part(plane, b):
        return rows.at[plane, pl.ds(b * per_block, per_block)]

    def y_copy(k, b):
        return pltpu.make_async_remote_copy(
            part(dp, b), part(dp, b), y_send.at[k, b], y_recv.at[k, b],
            device_id=at(lax.rem(here_y + k, n_y) * CORES + core, ce), device_id_type=MESH)

    def plane_of(k, which):
        return lax.rem(here_y + n_y - k, n_y) * CORES + which

    def y_arrival(k, b):
        plane = plane_of(k, core)
        return pltpu.make_async_copy(part(plane, b), part(plane, b), y_recv.at[k, b])

    def c_copy(k, b):
        plane = plane_of(k, core)
        return pltpu.make_async_remote_copy(
            part(plane, b), part(plane, b), c_send.at[k, b], c_recv.at[k, b],
            device_id=at(mate, ce), device_id_type=MESH)

    mine = ce // per_block
    for i in range(blocks):
        b = lax.rem(mine + blocks - i, blocks)
        loop(per_block, lambda q: a_arrival(b * per_block + q).wait())
        for k in range(1, n_y):
            y_copy(k, b).start()
        c_copy(0, b).start()
        if i == 0 and direct:
            for far in offsets(n_dp, n_cent):
                all_copy(*far).start()

    if direct:
        for far in offsets(n_dp, n_cent):
            all_copy(*far).wait_recv()
    else:
        loop(n_cent - 1, lambda k: cent_copy(k).wait_recv())
    got = stats[...]
    total = jnp.sum(got, axis=(0, 1))
    mean = total[0:1] / (n_dp * n_cent)
    apart = jnp.sum((got - mean) ** 2, axis=(0, 1))
    var = (total[1:2] + rows_here * apart[0:1]) / float(rows_here * n_dp * n_cent)
    inverse = lax.rsqrt(var + eps_value)

    loads[2 + n_tiles].wait()
    selector = (
        (lax.broadcasted_iota(jnp.int32, (16, width), 0) == 0)
        & (lax.broadcasted_iota(jnp.int32, (16, width), 1) == 0)
    ).astype(jnp.float32).astype(jnp.bfloat16)

    def sm_copy(step, plane):
        return pltpu.make_async_remote_copy(
            sm_out.at[step, plane], sm_in.at[step, plane],
            sm_send.at[step, plane], sm_recv.at[step, plane],
            device_id=at(mate, ce), device_id_type=MESH)

    n_sub = plane_rows // TILE
    sub_cents = TILE // cap

    def sub_rows(plane, t):
        return zrows[plane, t * TILE:(t + 1) * TILE]

    def normalise(plane, t):
        part = slice(t * sub_cents, (t + 1) * sub_cents)
        raw = rows[plane, part]
        own = stats[part, plane]
        scale = jnp.sqrt(own[:, 1:2] / rows_here + eps_value) * inverse
        shift = (own[:, 0:1] - mean) * inverse
        x = (raw.astype(jnp.float32) * scale + shift).astype(jnp.bfloat16)
        zrows[plane, t * TILE:(t + 1) * TILE] = x.reshape(TILE, width)
        flag = lax.dot_general(
            selector, raw.reshape(TILE, width), NT, preferred_element_type=jnp.float32)
        live[plane, :, t * TILE:(t + 1) * TILE] = (flag[0:1] < 0.5 * DEAD).astype(jnp.float32)

    def first_pass(step, plane, rounded, cnorm):
        for t in range(n_sub):
            lanes = slice(t * TILE, (t + 1) * TILE)
            if step == 0:
                normalise(plane, t)
            x = sub_rows(plane, t)
            s = lax.dot_general(rounded, x, NT, preferred_element_type=jnp.float32)
            s = s * (2.0 * beta_scale * LOG2E) - cnorm
            top = jnp.max(s, axis=0, keepdims=True)
            e = jnp.exp2(s - top)
            expo[plane, :, lanes] = e
            sm_out[step, plane, 0:1, lanes] = top
            sm_out[step, plane, 1:2, lanes] = jnp.sum(e, axis=0, keepdims=True)
        sm_copy(step, plane).start()

    def second_pass(step, plane, h, count, num, den):
        if h == 0:
            sm_copy(step, plane).wait_recv()
        for t in range(n_sub):
            lanes = slice(t * TILE, (t + 1) * TILE)
            m0, s0 = sm_out[step, plane, 0:1, lanes], sm_out[step, plane, 1:2, lanes]
            m1, s1 = sm_in[step, plane, 0:1, lanes], sm_in[step, plane, 1:2, lanes]
            top = jnp.maximum(m0, m1)
            own = jnp.exp2(m0 - top)
            total = s0 * own + s1 * jnp.exp2(m1 - top)
            r = (expo[plane, h * count:(h + 1) * count, lanes] * (own / total * live[plane, :, lanes])).astype(jnp.bfloat16)
            num = num + jnp.dot(r, sub_rows(plane, t), preferred_element_type=jnp.float32)
            den = den + jnp.sum(r.astype(jnp.float32), axis=1, keepdims=True)
        return num, den

    def all_planes(body, carry):
        if n_dp <= UNROLL:
            for k in range(n_y):
                for other in range(CORES):
                    carry = body(plane_of(k, core if other == 0 else 1 - core), carry)
            return carry
        return lax.fori_loop(
            0, n_dp, lambda i, c: body(plane_of(i // CORES, lax.rem(core + i, CORES)), c), carry)

    def final_copy(h):
        span = pl.ds(h * (half // FINAL), half // FINAL)
        return pltpu.make_async_remote_copy(
            cur.at[span], out_ref.at[core, span], f_send.at[h], f_recv.at[h],
            device_id=at(mate, ce), device_id_type=MESH)

    def keep_copy(h):
        span = pl.ds(h * (half // FINAL), half // FINAL)
        return pltpu.make_async_copy(cur.at[span], out_ref.at[core, span], k_sem.at[h])

    for step in range(STEPS):
        current = cur[...]
        rounded = current.astype(jnp.bfloat16)
        cnorm = (beta_scale * LOG2E) * jnp.sum(current * current, axis=1, keepdims=True)
        if step == 0:
            first_pass(step, plane_of(0, core), rounded, cnorm)
            for i in range(blocks):
                c_copy(0, lax.rem(mine + blocks - i, blocks)).wait_recv()
            first_pass(step, plane_of(0, 1 - core), rounded, cnorm)
            for k in range(1, n_y):
                for i in range(blocks):
                    b = lax.rem(mine + blocks - i, blocks)
                    y_arrival(k, b).wait()
                    c_copy(k, b).start()
                first_pass(step, plane_of(k, core), rounded, cnorm)
                for i in range(blocks):
                    c_copy(k, lax.rem(mine + blocks - i, blocks)).wait_recv()
                first_pass(step, plane_of(k, 1 - core), rounded, cnorm)
        else:
            all_planes(lambda plane, c: (first_pass(step, plane, rounded, cnorm), c)[1], 0)
        pieces = FINAL if step == STEPS - 1 else 1
        count = half // pieces
        for h in range(pieces):
            num = jnp.zeros((count, width), jnp.float32)
            den = jnp.zeros((count, 1), jnp.float32)
            num, den = all_planes(
                lambda plane, c: second_pass(step, plane, h, count, c[0], c[1]), (num, den))
            mine_now = slice(h * count, (h + 1) * count)
            cur[mine_now] = (num + prior_weight * cur[mine_now]) / (den + prior_weight)
            if step == STEPS - 1:
                final_copy(h).start()
                keep_copy(h).start()

    if direct:
        for far in offsets(n_dp, n_cent):
            all_copy(*far).wait_send()
    else:
        loop(n_dp - 1, lambda k: dp_copy(k).wait_send())
        loop(n_cent - 1, lambda k: cent_copy(k).wait_send())
    loop(n_cent - 1, lambda k: a_copy(k).wait_send())
    for k in range(n_y):
        for b in range(blocks):
            if k:
                y_copy(k, b).wait_send()
            c_copy(k, b).wait_send()
    for step in range(STEPS):
        loop(n_dp, lambda plane: sm_copy(step, plane).wait_send())
    for h in range(FINAL):
        keep_copy(h).wait()
        final_copy(h).wait()


def per_device(fragments, order, group_ids, w_first, w_second, centroids):
    rows_here, emb = fragments.shape
    hid, width = w_second.shape
    n_dp, n_cent = lax.axis_size("dp"), lax.axis_size("cent")
    n_y = n_dp // CORES
    cap = max(16, 2 * rows_here // n_cent)
    plane_rows = n_cent * cap
    blocks = min(n_cent, 8)
    half = centroids.shape[0] // CORES
    n_tiles = hid // TILE
    n_stat = n_dp * n_cent if n_dp * n_cent <= 32 else n_dp
    f32, bf16 = jnp.float32, jnp.bfloat16
    dma = pltpu.SemaphoreType.DMA
    hbm = pl.BlockSpec(memory_space=pltpu.HBM)
    out = pl.pallas_call(
        functools.partial(kernel, n_dp, n_cent, cap, blocks),
        out_shape=jax.ShapeDtypeStruct((CORES, half, width), f32),
        in_specs=[hbm] * 6,
        out_specs=hbm,
        scratch_shapes=[
            pltpu.VMEM((rows_here, emb), bf16),
            pltpu.VMEM((1, rows_here), jnp.int32),
            pltpu.VMEM((1, rows_here), jnp.int32),
            pltpu.VMEM((emb, hid), bf16),
            pltpu.VMEM((hid, width), bf16),
            pltpu.VMEM((half, width), f32),
            pltpu.VMEM((rows_here, width), f32),
            pltpu.VMEM((n_cent, cap, width), bf16),
            pltpu.VMEM((n_dp, n_cent, cap, width), bf16),
            pltpu.VMEM((n_dp, plane_rows, width), bf16),
            pltpu.VMEM((n_dp, half, plane_rows), f32),
            pltpu.VMEM((n_dp, 1, plane_rows), f32),
            pltpu.VMEM((STEPS, n_dp, 2, plane_rows), f32),
            pltpu.VMEM((STEPS, n_dp, 2, plane_rows), f32),
            pltpu.VMEM((n_cent, n_dp, 2, width), f32),
            dma((5 + n_tiles,)),
            dma((n_cent,)), dma((n_cent,)),
            dma((n_y, blocks)), dma((n_y, blocks)),
            dma((n_y, blocks)), dma((n_y, blocks)),
            dma((n_stat,)), dma((n_stat,)),
            dma((n_cent,)), dma((n_cent,)),
            dma((STEPS, n_dp)), dma((STEPS, n_dp)),
            dma((FINAL,)), dma((FINAL,)), dma((FINAL,)),
        ],
        compiler_params=pltpu.CompilerParams(
            collective_id=0, has_side_effects=True, vmem_limit_bytes=VMEM_BYTES
        ),
    )(
        fragments, order, group_ids.reshape(1, rows_here), w_first, w_second,
        centroids.reshape(CORES, half, width),
    )
    return out.reshape(CORES * half, width)


def solution(mesh):
    return jax.shard_map(
        per_device,
        mesh=mesh,
        in_specs=(
            P(("dp", "cent"), None),
            P(("dp", "cent"), None),
            P(("dp", "cent"), None),
            P(),
            P(),
            P("cent", None),
        ),
        out_specs=P("cent", None),
        check_vma=False,
    )
```

```python
import functools

import jax
import jax.numpy as jnp
from jax import lax
from jax.experimental import pallas as pl
from jax.experimental.pallas import tpu as pltpu
from jax.sharding import PartitionSpec as P

STEPS = 2
CORES = 2

beta_scale = 0.0625
prior_weight = 1.0
eps_value = 1e-05
LOG2E = 1.4426950408889634
DEAD = 1024.0
UNROLL = 8
TILE = 256
FINAL = 2
VMEM_BYTES = 60 << 20

MESH = pl.DeviceIdType.MESH
NT = (((1,), (1,)), ((), ()))


def loop(n, body):
    if n <= UNROLL:
        for i in range(n):
            body(i)
    else:
        lax.fori_loop(0, n, lambda i, c: (body(i), c)[1], 0)


def offsets(n_dp, n_cent):
    return [(a, b) for b in range(n_cent) for a in range(n_dp) if a or b]


def kernel(
    n_dp, n_cent, cap, blocks,
    frag_hbm, order_hbm, group_hbm, w1_hbm, w2_hbm, cent_hbm,
    out_ref,
    frag, order_ref, group_ref, w1, w2, cur, proj, packed, rows, zrows, expo, live, sm_out, sm_in, stats,
    in_sem, a_send, a_recv, y_send, y_recv, c_send, c_recv, s1_send, s1_recv, s2_send, s2_recv,
    sm_send, sm_recv, f_send, f_recv, k_sem,
):
    dp, ce = lax.axis_index("dp"), lax.axis_index("cent")
    core = lax.rem(dp, CORES)
    n_y = n_dp // CORES
    here_y = dp // CORES
    mate = here_y * CORES + (1 - core)
    rows_here, emb = frag.shape
    hid = w1.shape[1]
    width = w2.shape[1]
    half = cur.shape[0]
    per_block = n_cent // blocks
    plane_rows = n_cent * cap

    def at(d, c):
        return {"dp": d, "cent": c}

    n_tiles = hid // TILE
    small = [
        pltpu.make_async_copy(group_hbm, group_ref, in_sem.at[3 + n_tiles]),
        pltpu.make_async_copy(order_hbm, order_ref, in_sem.at[4 + n_tiles]),
    ]
    loads = [pltpu.make_async_copy(frag_hbm, frag, in_sem.at[0])]
    for j in range(n_tiles):
        cols = pl.ds(j * TILE, TILE)
        loads.append(pltpu.make_async_copy(w1_hbm.at[:, cols], w1.at[:, cols], in_sem.at[1 + j]))
    loads.append(pltpu.make_async_copy(w2_hbm, w2, in_sem.at[1 + n_tiles]))
    loads.append(pltpu.make_async_copy(cent_hbm.at[core], cur, in_sem.at[2 + n_tiles]))
    for c in small + loads:
        c.start()

    barrier = pltpu.get_barrier_semaphore()

    def greet_dp(k):
        pl.semaphore_signal(barrier, 1, device_id=at(lax.rem(dp + k + 1, n_dp), ce), device_id_type=MESH)

    def greet_cent(k):
        pl.semaphore_signal(barrier, 1, device_id=at(dp, lax.rem(ce + k + 1, n_cent)), device_id_type=MESH)

    direct = s1_send.shape[0] == n_dp * n_cent
    if direct:
        greeted = n_dp * n_cent - 1
        for a, b in offsets(n_dp, n_cent):
            pl.semaphore_signal(
                barrier, 1, device_id=at(lax.rem(dp + a, n_dp), lax.rem(ce + b, n_cent)),
                device_id_type=MESH)
    else:
        greeted = n_dp - 1 + n_cent - 1
        loop(n_dp - 1, greet_dp)
        loop(n_cent - 1, greet_cent)

    for c in small:
        c.wait()
    groups = group_ref[...]
    member = lax.broadcasted_iota(jnp.int32, (max(n_cent, 16), rows_here), 0) == groups
    memberf = member.astype(jnp.float32)
    earlier = (
        lax.broadcasted_iota(jnp.int32, (rows_here, rows_here), 0)
        < lax.broadcasted_iota(jnp.int32, (rows_here, rows_here), 1)
    ).astype(jnp.float32).astype(jnp.bfloat16)
    counts = jnp.dot(memberf.astype(jnp.bfloat16), earlier, preferred_element_type=jnp.float32)
    rank = jnp.sum(counts * memberf, axis=0, keepdims=True).astype(jnp.int32)
    slot = groups * cap + rank
    place = (
        lax.broadcasted_iota(jnp.int32, (plane_rows, rows_here), 0) == slot
    ).astype(jnp.float32).astype(jnp.bfloat16)
    taken = (
        lax.broadcasted_iota(jnp.int32, (rows_here, rows_here), 0) == order_ref[...]
    ).astype(jnp.float32).astype(jnp.bfloat16)
    pickf = lax.dot_general(place, taken, NT, preferred_element_type=jnp.float32)
    pick = pickf.astype(jnp.bfloat16)
    dead = DEAD * (1.0 - jnp.sum(pickf, axis=1, keepdims=True))
    mark = jnp.where(
        lax.broadcasted_iota(jnp.int32, (plane_rows, width), 1) == 0, dead, 0.0
    )

    loads[0].wait()
    loads[1 + n_tiles].wait()
    for j in range(n_tiles):
        loads[1 + j].wait()
        h = jnp.dot(frag[...], w1[:, j * TILE:(j + 1) * TILE], preferred_element_type=jnp.float32)
        h = jax.nn.gelu(h, approximate=True).astype(jnp.bfloat16)
        p = jnp.dot(h, w2[j * TILE:(j + 1) * TILE, :], preferred_element_type=jnp.float32)
        if j == 0:
            proj[...] = p
        else:
            proj[...] += p

    pr = proj[...]
    mean = jnp.sum(pr, axis=0, keepdims=True) / rows_here
    centered = pr - mean
    square = jnp.sum(centered * centered, axis=0, keepdims=True)
    stats[ce, dp, 0:1, :] = mean
    stats[ce, dp, 1:2, :] = square
    z = (centered * lax.rsqrt(square / rows_here + eps_value)).astype(jnp.bfloat16)
    full = jnp.dot(pick, z, preferred_element_type=jnp.float32) + mark
    packed[...] = full.astype(jnp.bfloat16).reshape(n_cent, cap, width)

    pl.semaphore_wait(barrier, greeted)

    def dp_copy(k):
        return pltpu.make_async_remote_copy(
            stats.at[ce, dp], stats.at[ce, dp], s1_send.at[k], s1_recv.at[k],
            device_id=at(lax.rem(dp + k + 1, n_dp), ce), device_id_type=MESH)

    def cent_copy(k):
        return pltpu.make_async_remote_copy(
            stats.at[ce], stats.at[ce], s2_send.at[k], s2_recv.at[k],
            device_id=at(dp, lax.rem(ce + k + 1, n_cent)), device_id_type=MESH)

    def all_copy(a, b):
        return pltpu.make_async_remote_copy(
            stats.at[ce, dp], stats.at[ce, dp], s1_send.at[a * n_cent + b], s1_recv.at[a * n_cent + b],
            device_id=at(lax.rem(dp + a, n_dp), lax.rem(ce + b, n_cent)), device_id_type=MESH)


    def a_copy(k):
        peer = lax.rem(ce + k + 1, n_cent)
        return pltpu.make_async_remote_copy(
            packed.at[peer], rows.at[dp, ce], a_send.at[peer], a_recv.at[ce],
            device_id=at(dp, peer), device_id_type=MESH)

    def a_arrival(src):
        return pltpu.make_async_copy(packed.at[src], rows.at[dp, src], a_recv.at[src])

    a_arrival(ce).start()
    loop(n_cent - 1, lambda k: a_copy(k).start())
    if not direct:
        loop(n_dp - 1, lambda k: dp_copy(k).start())
        loop(n_dp - 1, lambda k: dp_copy(k).wait_recv())
        loop(n_cent - 1, lambda k: cent_copy(k).start())

    def part(plane, b):
        return rows.at[plane, pl.ds(b * per_block, per_block)]

    def y_copy(k, b):
        return pltpu.make_async_remote_copy(
            part(dp, b), part(dp, b), y_send.at[k, b], y_recv.at[k, b],
            device_id=at(lax.rem(here_y + k, n_y) * CORES + core, ce), device_id_type=MESH)

    def plane_of(k, which):
        return lax.rem(here_y + n_y - k, n_y) * CORES + which

    def y_arrival(k, b):
        plane = plane_of(k, core)
        return pltpu.make_async_copy(part(plane, b), part(plane, b), y_recv.at[k, b])

    def c_copy(k, b):
        plane = plane_of(k, core)
        return pltpu.make_async_remote_copy(
            part(plane, b), part(plane, b), c_send.at[k, b], c_recv.at[k, b],
            device_id=at(mate, ce), device_id_type=MESH)

    mine = ce // per_block
    for i in range(blocks):
        b = lax.rem(mine + blocks - i, blocks)
        loop(per_block, lambda q: a_arrival(b * per_block + q).wait())
        for k in range(1, n_y):
            y_copy(k, b).start()
        c_copy(0, b).start()
        if i == 0 and direct:
            for far in offsets(n_dp, n_cent):
                all_copy(*far).start()

    if direct:
        for far in offsets(n_dp, n_cent):
            all_copy(*far).wait_recv()
    else:
        loop(n_cent - 1, lambda k: cent_copy(k).wait_recv())
    got = stats[...]
    total = jnp.sum(got, axis=(0, 1))
    mean = total[0:1] / (n_dp * n_cent)
    apart = jnp.sum((got - mean) ** 2, axis=(0, 1))
    var = (total[1:2] + rows_here * apart[0:1]) / float(rows_here * n_dp * n_cent)
    inverse = lax.rsqrt(var + eps_value)

    loads[2 + n_tiles].wait()
    selector = (
        (lax.broadcasted_iota(jnp.int32, (16, width), 0) == 0)
        & (lax.broadcasted_iota(jnp.int32, (16, width), 1) == 0)
    ).astype(jnp.float32).astype(jnp.bfloat16)

    def sm_copy(step, plane):
        return pltpu.make_async_remote_copy(
            sm_out.at[step, plane], sm_in.at[step, plane],
            sm_send.at[step, plane], sm_recv.at[step, plane],
            device_id=at(mate, ce), device_id_type=MESH)

    n_sub = plane_rows // TILE
    sub_cents = TILE // cap

    def sub_rows(plane, t):
        return zrows[plane, t * TILE:(t + 1) * TILE]

    def normalise(plane, t):
        part = slice(t * sub_cents, (t + 1) * sub_cents)
        raw = rows[plane, part]
        own = stats[part, plane]
        scale = jnp.sqrt(own[:, 1:2] / rows_here + eps_value) * inverse
        shift = (own[:, 0:1] - mean) * inverse
        x = (raw.astype(jnp.float32) * scale + shift).astype(jnp.bfloat16)
        zrows[plane, t * TILE:(t + 1) * TILE] = x.reshape(TILE, width)
        flag = lax.dot_general(
            selector, raw.reshape(TILE, width), NT, preferred_element_type=jnp.float32)
        live[plane, :, t * TILE:(t + 1) * TILE] = (flag[0:1] < 0.5 * DEAD).astype(jnp.float32)

    def first_pass(step, plane, rounded, cnorm):
        for t in range(n_sub):
            lanes = slice(t * TILE, (t + 1) * TILE)
            if step == 0:
                normalise(plane, t)
            x = sub_rows(plane, t)
            s = lax.dot_general(rounded, x, NT, preferred_element_type=jnp.float32)
            s = s * (2.0 * beta_scale * LOG2E) - cnorm
            top = jnp.max(s, axis=0, keepdims=True)
            e = jnp.exp2(s - top)
            expo[plane, :, lanes] = e
            sm_out[step, plane, 0:1, lanes] = top
            sm_out[step, plane, 1:2, lanes] = jnp.sum(e, axis=0, keepdims=True)
        sm_copy(step, plane).start()

    def second_pass(step, plane, h, count, num, den):
        if h == 0:
            sm_copy(step, plane).wait_recv()
        for t in range(n_sub):
            lanes = slice(t * TILE, (t + 1) * TILE)
            m0, s0 = sm_out[step, plane, 0:1, lanes], sm_out[step, plane, 1:2, lanes]
            m1, s1 = sm_in[step, plane, 0:1, lanes], sm_in[step, plane, 1:2, lanes]
            top = jnp.maximum(m0, m1)
            own = jnp.exp2(m0 - top)
            total = s0 * own + s1 * jnp.exp2(m1 - top)
            r = (expo[plane, h * count:(h + 1) * count, lanes] * (own / total * live[plane, :, lanes])).astype(jnp.bfloat16)
            num = num + jnp.dot(r, sub_rows(plane, t), preferred_element_type=jnp.float32)
            den = den + jnp.sum(r.astype(jnp.float32), axis=1, keepdims=True)
        return num, den

    def all_planes(body, carry):
        if n_dp <= UNROLL:
            for k in range(n_y):
                for other in range(CORES):
                    carry = body(plane_of(k, core if other == 0 else 1 - core), carry)
            return carry
        return lax.fori_loop(
            0, n_dp, lambda i, c: body(plane_of(i // CORES, lax.rem(core + i, CORES)), c), carry)

    def final_copy(h):
        span = pl.ds(h * (half // FINAL), half // FINAL)
        return pltpu.make_async_remote_copy(
            cur.at[span], out_ref.at[core, span], f_send.at[h], f_recv.at[h],
            device_id=at(mate, ce), device_id_type=MESH)

    def keep_copy(h):
        span = pl.ds(h * (half // FINAL), half // FINAL)
        return pltpu.make_async_copy(cur.at[span], out_ref.at[core, span], k_sem.at[h])

    for step in range(STEPS):
        current = cur[...]
        rounded = current.astype(jnp.bfloat16)
        cnorm = (beta_scale * LOG2E) * jnp.sum(current * current, axis=1, keepdims=True)
        if step == 0:
            first_pass(step, plane_of(0, core), rounded, cnorm)
            for i in range(blocks):
                c_copy(0, lax.rem(mine + blocks - i, blocks)).wait_recv()
            first_pass(step, plane_of(0, 1 - core), rounded, cnorm)
            for k in range(1, n_y):
                for i in range(blocks):
                    b = lax.rem(mine + blocks - i, blocks)
                    y_arrival(k, b).wait()
                    c_copy(k, b).start()
                first_pass(step, plane_of(k, core), rounded, cnorm)
                for i in range(blocks):
                    c_copy(k, lax.rem(mine + blocks - i, blocks)).wait_recv()
                first_pass(step, plane_of(k, 1 - core), rounded, cnorm)
        else:
            all_planes(lambda plane, c: (first_pass(step, plane, rounded, cnorm), c)[1], 0)
        pieces = FINAL if step == STEPS - 1 else 1
        count = half // pieces
        for h in range(pieces):
            num = jnp.zeros((count, width), jnp.float32)
            den = jnp.zeros((count, 1), jnp.float32)
            num, den = all_planes(
                lambda plane, c: second_pass(step, plane, h, count, c[0], c[1]), (num, den))
            mine_now = slice(h * count, (h + 1) * count)
            cur[mine_now] = (num + prior_weight * cur[mine_now]) / (den + prior_weight)
            if step == STEPS - 1:
                final_copy(h).start()
                keep_copy(h).start()

    if direct:
        for far in offsets(n_dp, n_cent):
            all_copy(*far).wait_send()
    else:
        loop(n_dp - 1, lambda k: dp_copy(k).wait_send())
        loop(n_cent - 1, lambda k: cent_copy(k).wait_send())
    loop(n_cent - 1, lambda k: a_copy(k).wait_send())
    for k in range(n_y):
        for b in range(blocks):
            if k:
                y_copy(k, b).wait_send()
            c_copy(k, b).wait_send()
    for step in range(STEPS):
        loop(n_dp, lambda plane: sm_copy(step, plane).wait_send())
    for h in range(FINAL):
        keep_copy(h).wait()
        final_copy(h).wait()


def per_device(fragments, order, group_ids, w_first, w_second, centroids):
    rows_here, emb = fragments.shape
    hid, width = w_second.shape
    n_dp, n_cent = lax.axis_size("dp"), lax.axis_size("cent")
    n_y = n_dp // CORES
    cap = max(16, 2 * rows_here // n_cent)
    plane_rows = n_cent * cap
    blocks = min(n_cent, 8)
    half = centroids.shape[0] // CORES
    n_tiles = hid // TILE
    n_stat = n_dp
    f32, bf16 = jnp.float32, jnp.bfloat16
    dma = pltpu.SemaphoreType.DMA
    hbm = pl.BlockSpec(memory_space=pltpu.HBM)
    out = pl.pallas_call(
        functools.partial(kernel, n_dp, n_cent, cap, blocks),
        out_shape=jax.ShapeDtypeStruct((CORES, half, width), f32),
        in_specs=[hbm] * 6,
        out_specs=hbm,
        scratch_shapes=[
            pltpu.VMEM((rows_here, emb), bf16),
            pltpu.VMEM((1, rows_here), jnp.int32),
            pltpu.VMEM((1, rows_here), jnp.int32),
            pltpu.VMEM((emb, hid), bf16),
            pltpu.VMEM((hid, width), bf16),
            pltpu.VMEM((half, width), f32),
            pltpu.VMEM((rows_here, width), f32),
            pltpu.VMEM((n_cent, cap, width), bf16),
            pltpu.VMEM((n_dp, n_cent, cap, width), bf16),
            pltpu.VMEM((n_dp, plane_rows, width), bf16),
            pltpu.VMEM((n_dp, half, plane_rows), f32),
            pltpu.VMEM((n_dp, 1, plane_rows), f32),
            pltpu.VMEM((STEPS, n_dp, 2, plane_rows), f32),
            pltpu.VMEM((STEPS, n_dp, 2, plane_rows), f32),
            pltpu.VMEM((n_cent, n_dp, 2, width), f32),
            dma((5 + n_tiles,)),
            dma((n_cent,)), dma((n_cent,)),
            dma((n_y, blocks)), dma((n_y, blocks)),
            dma((n_y, blocks)), dma((n_y, blocks)),
            dma((n_stat,)), dma((n_stat,)),
            dma((n_cent,)), dma((n_cent,)),
            dma((STEPS, n_dp)), dma((STEPS, n_dp)),
            dma((FINAL,)), dma((FINAL,)), dma((FINAL,)),
        ],
        compiler_params=pltpu.CompilerParams(
            collective_id=0, has_side_effects=True, vmem_limit_bytes=VMEM_BYTES
        ),
    )(
        fragments, order, group_ids.reshape(1, rows_here), w_first, w_second,
        centroids.reshape(CORES, half, width),
    )
    return out.reshape(CORES * half, width)


def solution(mesh):
    return jax.shard_map(
        per_device,
        mesh=mesh,
        in_specs=(
            P(("dp", "cent"), None),
            P(("dp", "cent"), None),
            P(("dp", "cent"), None),
            P(),
            P(),
            P("cent", None),
        ),
        out_specs=P("cent", None),
        check_vma=False,
    )
```
